32 devices in a mesh: gx: 4 (over y, core), gy: 8 (over z, x).
Axes of the slice: x: 2, y: 2, z: 4, core: 2. Of those that a mesh axis runs over, the one named last changes fastest.
Arguments:
- start_vector: float32 [2, 16, 64, 1024], P(None, None, 'gx', 'gy'), may hold values from -6 to 6
- viscosity: float32 [16, 64, 1024], P(None, 'gx', 'gy'), may hold values from 0.1 to 10
- friction: float32 [16, 64, 1024], P(None, 'gx', 'gy'), may hold values from 0.5 to 5
- shifts: float32 [8], replicated, may hold values from 0.2 to 1.6, as said below
Outputs:
- orthonormal: float32 [9, 2, 16, 64, 1024], P(None, None, None, 'gx', 'gy')
- factor: float32 [9, 9], replicated
The draws below stay inside these ranges and needn't reach their ends.
Inputs may be any that keep to these rules, and one draw needn't show every extreme that they name: The 8 shifts are distinct, one in each of 8 equal parts of the range.
All inputs are finite; a program needn't handle non-finite values.
Results may differ from the reference program's by a relative error of at most 0.00035.
Values sent between devices are 32-bit elements; how exact they have to be, the bound alone decides.
A program may use at most 128 MiB of HBM per device.

```python
import math
import jax
import jax.numpy as jnp
from jax import lax

NZ = 16
S = 8
NX = 64
NY = 1024
M = 2097152


def draw_start_vector(key, part):
    first_key = jax.random.fold_in(key, 11)
    shape_full = (2, NZ, NX, NY)
    values = jax.random.normal(first_key, shape_full, jnp.float32)
    return jnp.clip(values, -6.0, 6.0).astype(jnp.float32)


def draw_shifts(key, part):
    jitter_key = jax.random.fold_in(key, 21)
    order_key = jax.random.fold_in(key, 22)
    jitter = jax.random.uniform(jitter_key, (S,), jnp.float32, 0.1, 0.9)
    spaced = 0.2 + 1.4 * (jnp.arange(S).astype(jnp.float32) + jitter) / S
    order = jax.random.permutation(order_key, S)
    return spaced[order].astype(jnp.float32)


def steps_of(rng, shape, pieces, least, top_value):
    gain = 1.0
    for dim, parts in pieces:
        draws = jax.random.uniform(jax.random.fold_in(jax.random.fold_in(rng, 6), dim), (parts,), jnp.float32, least / len(pieces), top_value / len(pieces))
        gain = gain * jnp.repeat(jnp.exp(draws), shape[dim] // parts).reshape((-1,) + (1,) * (len(shape) - 1 - dim))
    return gain


def setup_inputs(seed: int = 0) -> dict:
    key_of = jax.random.split(jax.random.key(seed), 5)
    start_vector = draw_start_vector(jax.random.fold_in(key_of[4], 71), 0)
    viscosity = jnp.clip(jnp.exp(math.log(10.0) - 4.6051702 * jax.random.uniform(key_of[1], (NZ, NX, NY), jnp.float32) ** steps_of(key_of[1], (NZ, NX, NY), ((1, 4), (2, 8)), -0.2, 0.2)), 0.1, 10.0)
    friction = jnp.clip(jnp.exp(math.log(5.0) - 2.3025851 * jax.random.uniform(key_of[2], (NZ, NX, NY), jnp.float32) ** steps_of(key_of[2], (NZ, NX, NY), ((1, 4), (2, 8)), -0.2, 0.2)), 0.5, 5.0)
    shifts = draw_shifts(jax.random.fold_in(key_of[4], 71), 0)
    return dict(start_vector=start_vector, viscosity=viscosity, friction=friction, shifts=shifts)


cross_gain = 1.0

def neighbour_offsets():
    offsets = []
    for shift_z in (-1, 0, 1):
        for shift_x in (-1, 0, 1):
            for shift_y in (-1, 0, 1):
                distance = abs(shift_z) + abs(shift_x) + abs(shift_y)
                if distance == 0:
                    continue
                offsets.append((shift_z, shift_x, shift_y, 0.5 ** (distance - 1)))
    return offsets

def apply_operator(field_pad, eta_pad, friction, region_mask):
    levels = friction.shape[0]
    row_count = field_pad.shape[2] - 2
    col_count = field_pad.shape[3] - 2
    eta_z = jnp.pad(eta_pad, ((1, 1), (0, 0), (0, 0)))
    field_z = jnp.pad(field_pad, ((0, 0), (1, 1), (0, 0), (0, 0)))
    centre_eta = eta_pad[:, 1:1 + row_count, 1:1 + col_count]
    diagonal = friction
    summed = jnp.zeros((2, levels, row_count, col_count), jnp.float32)
    for shift_z, shift_x, shift_y, weight in neighbour_offsets():
        linkage = weight * 0.5 * (centre_eta + eta_z[1 + shift_z:1 + shift_z + levels, 1 + shift_x:1 + shift_x + row_count, 1 + shift_y:1 + shift_y + col_count])
        diagonal = diagonal + linkage
        summed = summed + linkage[None] * field_z[:, 1 + shift_z:1 + shift_z + levels, 1 + shift_x:1 + shift_x + row_count, 1 + shift_y:1 + shift_y + col_count]
    crossed = 0.25 * (field_pad[:, :, 2:2 + row_count, 2:2 + col_count] - field_pad[:, :, 2:2 + row_count, 0:col_count] - field_pad[:, :, 0:row_count, 2:2 + col_count] + field_pad[:, :, 0:row_count, 0:col_count])
    centre = field_pad[:, :, 1:1 + row_count, 1:1 + col_count]
    safe_diag = jnp.where(region_mask > 0, diagonal, 1.0)
    result = centre - (summed - cross_gain * centre_eta[None] * crossed[::-1]) / safe_diag
    return result * region_mask

def lower_inverse(factor_low):
    order_n = factor_low.shape[0]
    identity = jnp.eye(order_n, dtype=jnp.float32)
    inverse = jnp.zeros((order_n, order_n), jnp.float32)
    for position in range(order_n):
        earlier = jnp.dot(factor_low[position, :position], inverse[:position], precision=lax.Precision.HIGHEST)
        inverse = inverse.at[position].set((identity[position] - earlier) / factor_low[position, position])
    return inverse

def cholesky_pass(basis_rows, gram):
    factor_low = jnp.linalg.cholesky(gram)
    return (jnp.dot(lower_inverse(factor_low), basis_rows, precision=lax.Precision.HIGHEST), factor_low)

def reference(start_vector, viscosity, friction, shifts):
    current = start_vector
    krylov = [start_vector]
    eta_pad = jnp.pad(viscosity, ((0, 0), (1, 1), (1, 1)))
    for power in range(S):
        padded = jnp.pad(current, ((0, 0), (0, 0), (1, 1), (1, 1)))
        current = apply_operator(padded, eta_pad, friction, 1.0) - shifts[power] * current
        krylov.append(current)
    basis_rows = jnp.stack(krylov).reshape(S + 1, -1)
    gram_one = jnp.dot(basis_rows, basis_rows.T, precision=lax.Precision.HIGHEST) / M
    ortho_one, low_one = cholesky_pass(basis_rows, gram_one)
    gram_two = jnp.dot(ortho_one, ortho_one.T, precision=lax.Precision.HIGHEST) / M
    ortho_two, low_two = cholesky_pass(ortho_one, gram_two)
    factor = jnp.dot(low_two.T, low_one.T, precision=lax.Precision.HIGHEST)
    return (ortho_two.reshape(S + 1, 2, NZ, NX, NY), factor)
```

```python
import functools

import jax
import jax.numpy as jnp
from jax import lax
from jax.experimental import pallas as pl
from jax.experimental.pallas import tpu as pltpu
from jax.sharding import PartitionSpec as P

MESH = pl.DeviceIdType.MESH
HALO = 8
GROUP = 2 * HALO
DIRECTIONS = ((1, 0), (-1, 0), (0, 1), (0, -1), (1, 1), (1, -1), (-1, 1), (-1, -1))


def both(lower_ok, upper_ok):
    if lower_ok is None:
        return upper_ok
    if upper_ok is None:
        return lower_ok
    return jnp.logical_and(lower_ok, upper_ok)


def kernel(
    gx_count,
    gy_count,
    start_ref,
    eta_in_ref,
    fric_in_ref,
    shift_ref,
    out_ref,
    factor_ref,
    cur,
    eta,
    fric,
    centre_coef,
    a_mid,
    g_mid,
    a_up,
    g_up,
    a_down,
    g_down,
    packed,
    edge,
    red,
    mine_x,
    mine_y,
    slots_x,
    slots_y,
    splat,
    lower_inv,
    row_send,
    row_recv,
    pack_send,
    pack_recv,
    gx_send,
    gx_recv,
    gy_send,
    gy_recv,
):
    powers = shift_ref.shape[0]
    count = powers + 1
    levels, rows, lanes = eta_in_ref.shape
    wide = rows + 2 * HALO
    me_x, me_y = lax.axis_index("gx"), lax.axis_index("gy")
    total_count = 2.0 * levels * rows * lanes * gx_count * gy_count

    def exists(dx, dy):
        x_ok = {1: me_x < gx_count - 1, -1: me_x > 0, 0: None}[dx]
        y_ok = {1: me_y < gy_count - 1, -1: me_y > 0, 0: None}[dy]
        return both(x_ok, y_ok)

    def device(dx, dy):
        return (jnp.clip(me_x + dx, 0, gx_count - 1), jnp.clip(me_y + dy, 0, gy_count - 1))

    def ring_x(step):
        return (lax.rem(me_x + step, gx_count), me_y)

    def ring_y(step):
        return (me_x, lax.rem(me_y + step, gy_count))

    barrier = pltpu.get_barrier_semaphore()
    for step in range(1, gx_count):
        pl.semaphore_signal(barrier, inc=1, device_id=ring_x(step), device_id_type=MESH)
    for step in range(1, gy_count):
        pl.semaphore_signal(barrier, inc=1, device_id=ring_y(step), device_id_type=MESH)
    for dx, dy in DIRECTIONS[4:]:

        @pl.when(exists(dx, dy))
        def _():
            pl.semaphore_signal(barrier, inc=1, device_id=device(dx, dy), device_id_type=MESH)

    lane = lax.broadcasted_iota(jnp.int32, (wide, lanes), 1)
    row = lax.broadcasted_iota(jnp.int32, (wide, lanes), 0)
    lane_in = lane[:rows]

    def source(field, level):
        if field < 2:
            return start_ref[field, level]
        return (eta_in_ref, fric_in_ref)[field - 2][level]

    for field in range(4):
        for group in range(levels // 8):
            tile = jnp.zeros((rows, lanes), jnp.float32)
            for inner in range(8):
                turned = pltpu.roll(
                    source(field, group * 8 + inner), (GROUP * inner + HALO) % lanes, 1
                )
                tile = jnp.where(lane_in // GROUP == inner, turned, tile)
            packed[field * (levels // 8) + group] = tile

    barrier_x = jnp.where(me_x > 0, 1, 0) + jnp.where(me_x < gx_count - 1, 1, 0)
    barrier_y = jnp.where(me_y > 0, 1, 0) + jnp.where(me_y < gy_count - 1, 1, 0)
    pl.semaphore_wait(barrier, gx_count + gy_count - 2 + barrier_x * barrier_y)

    def row_copies(index):
        dx, dy = DIRECTIONS[index]
        src = pl.ds(rows - HALO, HALO) if dx > 0 else pl.ds(0, HALO)
        dst = pl.ds(0, HALO) if dx > 0 else pl.ds(rows + HALO, HALO)
        inner = pl.ds(1, levels)
        pairs = (
            (start_ref.at[:, :, src], cur.at[0, 0, :, inner, dst]),
            (eta_in_ref.at[:, src], eta.at[0, inner, dst]),
            (fric_in_ref.at[:, src], fric.at[0, :, dst]),
        )
        return [
            pltpu.make_async_remote_copy(
                src_ref=a,
                dst_ref=b,
                send_sem=row_send.at[index, n],
                recv_sem=row_recv.at[index, n],
                device_id=device(dx, dy),
                device_id_type=MESH,
            )
            for n, (a, b) in enumerate(pairs)
        ]

    def pack_copies(index):
        dx, dy = DIRECTIONS[index]
        side = 0 if dy > 0 else 1
        if dx == 0:
            src, dst = pl.ds(0, rows), pl.ds(HALO, rows)
        elif dx > 0:
            src, dst = pl.ds(rows - HALO, HALO), pl.ds(0, HALO)
        else:
            src, dst = pl.ds(0, HALO), pl.ds(rows + HALO, HALO)
        return [
            pltpu.make_async_remote_copy(
                src_ref=packed.at[:, src],
                dst_ref=edge.at[side, :, dst],
                send_sem=pack_send.at[index - 2],
                recv_sem=pack_recv.at[index - 2],
                device_id=device(dx, dy),
                device_id_type=MESH,
            )
        ]

    def copies(index):
        return row_copies(index) if index < 2 else pack_copies(index)

    for index, (dx, dy) in enumerate(DIRECTIONS):

        @pl.when(exists(dx, dy))
        def _():
            for copy in copies(index):
                copy.start()

    zero_tile = jnp.zeros((wide, lanes), jnp.float32)
    for comp in range(2):
        for tile in range(2):
            for slot in range(2):
                cur[slot, tile, comp, 0] = zero_tile
                cur[slot, tile, comp, levels + 1] = zero_tile
        cur[0, 0, comp, 1 : levels + 1, HALO : HALO + rows] = start_ref[comp]
        out_ref[0, comp] = start_ref[comp]
    for tile in range(2):
        eta[tile, 0] = zero_tile
        eta[tile, levels + 1] = zero_tile
    eta[0, 1 : levels + 1, HALO : HALO + rows] = eta_in_ref[...]
    fric[0, :, HALO : HALO + rows] = fric_in_ref[...]
    for index, (dx, dy) in enumerate(DIRECTIONS):
        here = exists(-dx, -dy)

        @pl.when(jnp.logical_not(here))
        def _():
            start = 0 if dx > 0 else (HALO if dx == 0 else rows + HALO)
            size = rows if dx == 0 else HALO
            if dy == 0:
                blank = jnp.zeros((levels, HALO, lanes), jnp.float32)
                for comp in range(2):
                    cur[0, 0, comp, 1 : levels + 1, start : start + size] = blank
                eta[0, 1 : levels + 1, start : start + size] = blank
                fric[0, :, start : start + size] = blank
            else:
                side = 0 if dy > 0 else 1
                edge[side, :, start : start + size] = jnp.zeros(
                    (edge.shape[1], size, lanes), jnp.float32
                )

        @pl.when(here)
        def _():
            for copy in copies(index):
                copy.wait_recv()

    is_edge = (lane < HALO) | (lane >= lanes - HALO)
    for field in range(4):
        for group in range(levels // 8):
            spot = field * (levels // 8) + group
            merged = jnp.where(lane % GROUP >= HALO, edge[1, spot], edge[0, spot])
            for inner in range(8):
                level = group * 8 + inner
                turned = pltpu.roll(merged, (2 * lanes - GROUP * inner - HALO) % lanes, 1)
                turned = jnp.where(is_edge, turned, 0.0)
                if field < 2:
                    cur[0, 1, field, level + 1] = turned
                elif field == 2:
                    eta[1, level + 1] = turned
                else:
                    fric[1, level] = turned

    def from_next(first, second):
        a, b = pltpu.roll(first, lanes - 1, 1), pltpu.roll(second, lanes - 1, 1)
        return jnp.where(lane == lanes - 1, b, a), jnp.where(lane == lanes - 1, a, b)

    def from_last(first, second):
        a, b = pltpu.roll(first, 1, 1), pltpu.roll(second, 1, 1)
        return jnp.where(lane == 0, b, a), jnp.where(lane == 0, a, b)

    def smooth_rows(value):
        pair = value + pltpu.roll(value, wide - 1, 0)
        return pair + pltpu.roll(pair, 1, 0)

    row_ok = ((row >= HALO) | (me_x > 0)) & ((row < HALO + rows) | (me_x < gx_count - 1))
    side_ok = ((lane < HALO) & (me_y < gy_count - 1)) | ((lane >= lanes - HALO) & (me_y > 0))
    inside = (row_ok, row_ok & side_ok)

    def coefficients(level, carry):
        sums = [
            smooth_rows(eta[t, level] + 2.0 * eta[t, level + 1] + eta[t, level + 2])
            for t in range(2)
        ]
        after, before = from_next(*sums), from_last(*sums)
        a_pair, g_pair = [], []
        for t in range(2):
            here = eta[t, level + 1]
            diagonal = (
                fric[t, level] + 6.0 * here + 0.125 * (2.0 * sums[t] + after[t] + before[t])
            )
            inverse = jnp.where(inside[t], 0.125 / jnp.where(inside[t], diagonal, 1.0), 0.0)
            a_pair.append(here * inverse)
            g_pair.append(inverse)
            centre_coef[t, level] = 1.0 + 16.0 * a_pair[t]
            a_mid[t, level] = 2.0 * a_pair[t]
            g_mid[t, level] = 2.0 * g_pair[t]
        for values, up, down in ((a_pair, a_up, a_down), (g_pair, g_up, g_down)):
            ahead, behind = from_last(*values), from_next(*values)
            for t in range(2):
                up[t, level] = ahead[t]
                down[t, level] = behind[t]
        return carry

    lax.fori_loop(0, levels, coefficients, 0)

    def power_step(power, carry):
        slot = lax.rem(power, 2)
        newton = shift_ref[power]

        def level_step(level, inner_carry):
            crossed = [[None, None], [None, None]]
            for t in range(2):
                for comp in range(2):
                    value = cur[slot, t, comp, level + 1]
                    slope = pltpu.roll(value, wide - 1, 0) - pltpu.roll(value, 1, 0)
                    crossed[comp][t] = slope + slope
            for comp in range(2):
                centre, ups, downs = [], [], []
                for t in range(2):
                    below = cur[slot, t, comp, level]
                    value = cur[slot, t, comp, level + 1]
                    above = cur[slot, t, comp, level + 2]
                    plain = smooth_rows(below + 2.0 * value + above)
                    scaled = smooth_rows(
                        eta[t, level] * below
                        + 2.0 * (eta[t, level + 1] * value)
                        + eta[t, level + 2] * above
                    )
                    cross = crossed[1 - comp][t]
                    centre.append(
                        (centre_coef[t, level] - newton) * value
                        - (a_mid[t, level] * plain + g_mid[t, level] * scaled)
                    )
                    ups.append(a_up[t, level] * (plain - cross) + g_up[t, level] * scaled)
                    downs.append(a_down[t, level] * (plain + cross) + g_down[t, level] * scaled)
                after, before = from_next(*ups), from_last(*downs)
                for t in range(2):
                    result = centre[t] - (after[t] + before[t])
                    cur[1 - slot, t, comp, level + 1] = result
                    if t == 0:
                        out_ref[power + 1, comp, level] = result[HALO : HALO + rows]
            return inner_carry

        return lax.fori_loop(0, levels, level_step, carry)

    lax.fori_loop(0, powers, power_step, 0)

    pairs = [(i, j) for i in range(count) for j in range(i + 1)]
    place = {pair: n for n, pair in enumerate(pairs)}
    tiles = (len(pairs) + 7) // 8
    lane_8 = lax.broadcasted_iota(jnp.int32, (8, lanes), 1)

    def add_products(sums, vectors):
        return tuple(total + vectors[i] * vectors[j] for total, (i, j) in zip(sums, pairs))

    zeros = tuple(jnp.zeros((8, lanes), jnp.float32) for _ in pairs)

    def exchange(phase, mine, slots, sends, recvs, me, peers, target):
        copies_out = []
        for step in range(1, peers):
            copy = pltpu.make_async_remote_copy(
                src_ref=mine.at[phase],
                dst_ref=slots.at[phase, me],
                send_sem=sends.at[phase, step],
                recv_sem=recvs.at[phase, step],
                device_id=target(step),
                device_id_type=MESH,
            )
            copy.start()
            copies_out.append(copy)
        slots[phase, me] = mine[phase]
        for copy in copies_out:
            copy.wait()
        total = slots[phase, 0]
        for peer in range(1, peers):
            total = total + slots[phase, peer]
        return total

    def gram_of(sums, phase):
        red[8 * tiles - 8 : 8 * tiles] = jnp.zeros((8, lanes), jnp.float32)
        for n, total in enumerate(sums):
            red[n : n + 1] = jnp.sum(total, axis=0, keepdims=True)
        summed = jnp.sum(red[...], axis=1, keepdims=True)
        tile = jnp.zeros((8, lanes), jnp.float32)
        for t in range(tiles):
            tile = jnp.where(lane_8 == t, summed[8 * t : 8 * t + 8], tile)
        mine_x[phase] = tile
        mine_y[phase] = exchange(
            phase, mine_x, slots_x, gx_send, gx_recv, me_x, gx_count, ring_x
        )
        whole = exchange(phase, mine_y, slots_y, gy_send, gy_recv, me_y, gy_count, ring_y)
        whole = whole / total_count
        for t in range(tiles):
            splat[8 * t : 8 * t + 8] = jnp.broadcast_to(whole[:, t : t + 1], (8, lanes))
        return {pair: splat[n : n + 1] for n, pair in enumerate(pairs)}

    def factorise(gram):
        left = dict(gram)
        low, inv = {}, {}
        for j in range(count):
            root = jnp.sqrt(left[j, j])
            scale = 1.0 / root
            low[j, j], inv[j, j] = root, scale
            for i in range(j + 1, count):
                low[i, j] = left[i, j] * scale
            for i in range(j + 1, count):
                for k in range(j + 1, i + 1):
                    left[i, k] = left[i, k] - low[i, j] * low[k, j]
        for i in range(count):
            for j in range(i):
                total = low[i, j] * inv[j, j]
                for k in range(j + 1, i):
                    total = total + low[i, k] * inv[k, j]
                inv[i, j] = -(total * inv[i, i])
        for pair, n in place.items():
            lower_inv[n : n + 1] = inv[pair]
        return low

    def combine(vectors):
        results = []
        for i in range(count):
            total = lower_inv[place[i, 0] : place[i, 0] + 1] * vectors[0]
            for j in range(1, i + 1):
                total = total + lower_inv[place[i, j] : place[i, j] + 1] * vectors[j]
            results.append(total)
        return results

    def basis_at(spot, half):
        comp, level = spot // levels, lax.rem(spot, levels)
        return [out_ref[n, comp, level, 8 * half : 8 * half + 8] for n in range(count)]

    def gram_step(spot, sums):
        for half in range(rows // 8):
            sums = add_products(sums, basis_at(spot, half))
        return sums

    low_one = factorise(gram_of(lax.fori_loop(0, 2 * levels, gram_step, zeros), 0))

    def ortho_step(spot, sums):
        comp, level = spot // levels, lax.rem(spot, levels)
        for half in range(rows // 8):
            vectors = combine(basis_at(spot, half))
            for n in range(count):
                out_ref[n, comp, level, 8 * half : 8 * half + 8] = vectors[n]
            sums = add_products(sums, vectors)
        return sums

    low_two = factorise(gram_of(lax.fori_loop(0, 2 * levels, ortho_step, zeros), 1))

    def last_step(spot, carry):
        comp, level = spot // levels, lax.rem(spot, levels)
        for half in range(rows // 8):
            vectors = combine(basis_at(spot, half))
            for n in range(count):
                out_ref[n, comp, level, 8 * half : 8 * half + 8] = vectors[n]
        return carry

    lax.fori_loop(0, 2 * levels, last_step, 0)

    fac_row = lax.broadcasted_iota(jnp.int32, (count, count), 0)
    fac_col = lax.broadcasted_iota(jnp.int32, (count, count), 1)
    factor = jnp.zeros((count, count), jnp.float32)
    for i in range(count):
        for j in range(i, count):
            total = low_two[i, i] * low_one[j, i]
            for k in range(i + 1, j + 1):
                total = total + low_two[k, i] * low_one[j, k]
            factor = jnp.where((fac_row == i) & (fac_col == j), total[:, :count], factor)
    factor_ref[...] = factor

    for index, (dx, dy) in enumerate(DIRECTIONS):

        @pl.when(exists(dx, dy))
        def _():
            for copy in copies(index):
                copy.wait_send()


def on_device(gx_count, gy_count, start_vector, viscosity, friction, shifts):
    levels, rows, lanes = viscosity.shape
    count = shifts.shape[0] + 1
    wide = rows + 2 * HALO
    tiles = (count * (count + 1) // 2 + 7) // 8
    f32 = jnp.float32
    coef = pltpu.VMEM((2, levels, wide, lanes), f32)
    dma = pltpu.SemaphoreType.DMA
    vmem = pl.BlockSpec(memory_space=pltpu.VMEM)
    return pl.pallas_call(
        functools.partial(kernel, gx_count, gy_count),
        out_shape=(
            jax.ShapeDtypeStruct((count,) + start_vector.shape, f32),
            jax.ShapeDtypeStruct((count, count), f32),
        ),
        in_specs=[vmem, vmem, vmem, pl.BlockSpec(memory_space=pltpu.SMEM)],
        out_specs=(vmem, vmem),
        scratch_shapes=[
            pltpu.VMEM((2, 2, 2, levels + 2, wide, lanes), f32),
            pltpu.VMEM((2, levels + 2, wide, lanes), f32),
            coef,
            coef,
            coef,
            coef,
            coef,
            coef,
            coef,
            coef,
            pltpu.VMEM((levels // 2, rows, lanes), f32),
            pltpu.VMEM((2, levels // 2, wide, lanes), f32),
            pltpu.VMEM((8 * tiles, lanes), f32),
            pltpu.VMEM((2, 8, lanes), f32),
            pltpu.VMEM((2, 8, lanes), f32),
            pltpu.VMEM((2, gx_count, 8, lanes), f32),
            pltpu.VMEM((2, gy_count, 8, lanes), f32),
            pltpu.VMEM((8 * tiles, lanes), f32),
            pltpu.VMEM((8 * tiles, lanes), f32),
            dma((2, 3)),
            dma((2, 3)),
            dma((6,)),
            dma((6,)),
            dma((2, gx_count)),
            dma((2, gx_count)),
            dma((2, gy_count)),
            dma((2, gy_count)),
        ],
        compiler_params=pltpu.CompilerParams(
            collective_id=0, has_side_effects=True, vmem_limit_bytes=40 * 2**20
        ),
    )(start_vector, viscosity, friction, shifts)


def solution(mesh):
    return jax.shard_map(
        functools.partial(on_device, mesh.shape["gx"], mesh.shape["gy"]),
        mesh=mesh,
        in_specs=(P(None, None, "gx", "gy"), P(None, "gx", "gy"), P(None, "gx", "gy"), P()),
        out_specs=(P(None, None, None, "gx", "gy"), P()),
        check_vma=False,
    )
```

```python
import functools

import jax
import jax.numpy as jnp
from jax import lax
from jax.experimental import pallas as pl
from jax.experimental.pallas import tpu as pltpu
from jax.sharding import PartitionSpec as P

MESH = pl.DeviceIdType.MESH
HALO = 8
GROUP = 2 * HALO
DIRECTIONS = ((1, 0), (-1, 0), (0, 1), (0, -1), (1, 1), (1, -1), (-1, 1), (-1, -1))


def both(lower_ok, upper_ok):
    if lower_ok is None:
        return upper_ok
    if upper_ok is None:
        return lower_ok
    return jnp.logical_and(lower_ok, upper_ok)


def kernel(
    gx_count,
    gy_count,
    start_ref,
    eta_in_ref,
    fric_in_ref,
    shift_ref,
    out_ref,
    factor_ref,
    cur,
    eta,
    fric,
    centre_coef,
    a_mid,
    g_mid,
    a_up,
    g_up,
    a_down,
    g_down,
    packed,
    edge,
    red,
    mine_x,
    mine_y,
    slots_x,
    slots_y,
    splat,
    lower_inv,
    row_send,
    row_recv,
    pack_send,
    pack_recv,
    gx_send,
    gx_recv,
    gy_send,
    gy_recv,
):
    powers = shift_ref.shape[0]
    count = powers + 1
    levels, rows, lanes = eta_in_ref.shape
    wide = rows + 2 * HALO
    me_x, me_y = lax.axis_index("gx"), lax.axis_index("gy")
    total_count = 2.0 * levels * rows * lanes * gx_count * gy_count

    def exists(dx, dy):
        x_ok = {1: me_x < gx_count - 1, -1: me_x > 0, 0: None}[dx]
        y_ok = {1: me_y < gy_count - 1, -1: me_y > 0, 0: None}[dy]
        return both(x_ok, y_ok)

    def device(dx, dy):
        return (jnp.clip(me_x + dx, 0, gx_count - 1), jnp.clip(me_y + dy, 0, gy_count - 1))

    def ring_x(step):
        return (lax.rem(me_x + step, gx_count), me_y)

    def ring_y(step):
        return (me_x, lax.rem(me_y + step, gy_count))

    barrier = pltpu.get_barrier_semaphore()
    for step in range(1, gx_count):
        pl.semaphore_signal(barrier, inc=1, device_id=ring_x(step), device_id_type=MESH)
    for step in range(1, gy_count):
        pl.semaphore_signal(barrier, inc=1, device_id=ring_y(step), device_id_type=MESH)
    for dx, dy in DIRECTIONS[4:]:

        @pl.when(exists(dx, dy))
        def _():
            pl.semaphore_signal(barrier, inc=1, device_id=device(dx, dy), device_id_type=MESH)

    lane = lax.broadcasted_iota(jnp.int32, (wide, lanes), 1)
    row = lax.broadcasted_iota(jnp.int32, (wide, lanes), 0)
    lane_in = lane[:rows]

    def source(field, level):
        if field < 2:
            return start_ref[field, level]
        return (eta_in_ref, fric_in_ref)[field - 2][level]

    for field in range(4):
        for group in range(levels // 8):
            tile = jnp.zeros((rows, lanes), jnp.float32)
            for inner in range(8):
                turned = pltpu.roll(
                    source(field, group * 8 + inner), (GROUP * inner + HALO) % lanes, 1
                )
                tile = jnp.where(lane_in // GROUP == inner, turned, tile)
            packed[field * (levels // 8) + group] = tile

    barrier_x = jnp.where(me_x > 0, 1, 0) + jnp.where(me_x < gx_count - 1, 1, 0)
    barrier_y = jnp.where(me_y > 0, 1, 0) + jnp.where(me_y < gy_count - 1, 1, 0)
    pl.semaphore_wait(barrier, gx_count + gy_count - 2 + barrier_x * barrier_y)

    def row_copies(index):
        dx, dy = DIRECTIONS[index]
        src = pl.ds(rows - HALO, HALO) if dx > 0 else pl.ds(0, HALO)
        dst = pl.ds(0, HALO) if dx > 0 else pl.ds(rows + HALO, HALO)
        inner = pl.ds(1, levels)
        pairs = (
            (start_ref.at[:, :, src], cur.at[0, 0, :, inner, dst]),
            (eta_in_ref.at[:, src], eta.at[0, inner, dst]),
            (fric_in_ref.at[:, src], fric.at[0, :, dst]),
        )
        return [
            pltpu.make_async_remote_copy(
                src_ref=a,
                dst_ref=b,
                send_sem=row_send.at[index, n],
                recv_sem=row_recv.at[index, n],
                device_id=device(dx, dy),
                device_id_type=MESH,
            )
            for n, (a, b) in enumerate(pairs)
        ]

    def pack_copies(index):
        dx, dy = DIRECTIONS[index]
        side = 0 if dy > 0 else 1
        if dx == 0:
            src, dst = pl.ds(0, rows), pl.ds(HALO, rows)
        elif dx > 0:
            src, dst = pl.ds(rows - HALO, HALO), pl.ds(0, HALO)
        else:
            src, dst = pl.ds(0, HALO), pl.ds(rows + HALO, HALO)
        return [
            pltpu.make_async_remote_copy(
                src_ref=packed.at[:, src],
                dst_ref=edge.at[side, :, dst],
                send_sem=pack_send.at[index - 2],
                recv_sem=pack_recv.at[index - 2],
                device_id=device(dx, dy),
                device_id_type=MESH,
            )
        ]

    def copies(index):
        return row_copies(index) if index < 2 else pack_copies(index)

    for index, (dx, dy) in enumerate(DIRECTIONS):

        @pl.when(exists(dx, dy))
        def _():
            for copy in copies(index):
                copy.start()

    zero_tile = jnp.zeros((wide, lanes), jnp.float32)
    for comp in range(2):
        for tile in range(2):
            for slot in range(2):
                cur[slot, tile, comp, 0] = zero_tile
                cur[slot, tile, comp, levels + 1] = zero_tile
        cur[0, 0, comp, 1 : levels + 1, HALO : HALO + rows] = start_ref[comp]
        out_ref[0, comp] = start_ref[comp]
    for tile in range(2):
        eta[tile, 0] = zero_tile
        eta[tile, levels + 1] = zero_tile
    eta[0, 1 : levels + 1, HALO : HALO + rows] = eta_in_ref[...]
    fric[0, :, HALO : HALO + rows] = fric_in_ref[...]
    for index, (dx, dy) in enumerate(DIRECTIONS):
        here = exists(-dx, -dy)

        @pl.when(jnp.logical_not(here))
        def _():
            start = 0 if dx > 0 else (HALO if dx == 0 else rows + HALO)
            size = rows if dx == 0 else HALO
            if dy == 0:
                blank = jnp.zeros((levels, HALO, lanes), jnp.float32)
                for comp in range(2):
                    cur[0, 0, comp, 1 : levels + 1, start : start + size] = blank
                eta[0, 1 : levels + 1, start : start + size] = blank
                fric[0, :, start : start + size] = blank
            else:
                side = 0 if dy > 0 else 1
                edge[side, :, start : start + size] = jnp.zeros(
                    (edge.shape[1], size, lanes), jnp.float32
                )

        @pl.when(here)
        def _():
            for copy in copies(index):
                copy.wait_recv()

    is_edge = (lane < HALO) | (lane >= lanes - HALO)
    for field in range(4):
        for group in range(levels // 8):
            spot = field * (levels // 8) + group
            merged = jnp.where(lane % GROUP >= HALO, edge[1, spot], edge[0, spot])
            for inner in range(8):
                level = group * 8 + inner
                turned = pltpu.roll(merged, (2 * lanes - GROUP * inner - HALO) % lanes, 1)
                turned = jnp.where(is_edge, turned, 0.0)
                if field < 2:
                    cur[0, 1, field, level + 1] = turned
                elif field == 2:
                    eta[1, level + 1] = turned
                else:
                    fric[1, level] = turned

    def from_next(first, second):
        a, b = pltpu.roll(first, lanes - 1, 1), pltpu.roll(second, lanes - 1, 1)
        at_end = lane[: first.shape[0]] == lanes - 1
        return jnp.where(at_end, b, a), jnp.where(at_end, a, b)

    def from_last(first, second):
        a, b = pltpu.roll(first, 1, 1), pltpu.roll(second, 1, 1)
        at_start = lane[: first.shape[0]] == 0
        return jnp.where(at_start, b, a), jnp.where(at_start, a, b)

    def smooth_rows(value):
        pair = value + pltpu.roll(value, wide - 1, 0)
        return pair + pltpu.roll(pair, 1, 0)

    row_ok = ((row >= HALO) | (me_x > 0)) & ((row < HALO + rows) | (me_x < gx_count - 1))
    side_ok = ((lane < HALO) & (me_y < gy_count - 1)) | ((lane >= lanes - HALO) & (me_y > 0))
    inside = (row_ok, row_ok & side_ok)

    def coefficients(level, carry):
        sums = [
            smooth_rows(eta[t, level] + 2.0 * eta[t, level + 1] + eta[t, level + 2])
            for t in range(2)
        ]
        after, before = from_next(*sums), from_last(*sums)
        a_pair, g_pair = [], []
        for t in range(2):
            here = eta[t, level + 1]
            diagonal = (
                fric[t, level] + 6.0 * here + 0.125 * (2.0 * sums[t] + after[t] + before[t])
            )
            inverse = jnp.where(inside[t], 0.125 / jnp.where(inside[t], diagonal, 1.0), 0.0)
            a_pair.append(here * inverse)
            g_pair.append(inverse)
            centre_coef[t, level] = 1.0 + 16.0 * a_pair[t]
            a_mid[t, level] = 2.0 * a_pair[t]
            g_mid[t, level] = 2.0 * g_pair[t]
        for values, up, down in ((a_pair, a_up, a_down), (g_pair, g_up, g_down)):
            ahead, behind = from_last(*values), from_next(*values)
            for t in range(2):
                up[t, level] = ahead[t]
                down[t, level] = behind[t]
        return carry

    lax.fori_loop(0, levels, coefficients, 0)

    def power_step(power, carry, final=False):
        kept = slice(HALO, HALO + rows) if final else slice(0, wide)

        slot = power % 2
        newton = shift_ref[power]

        def level_step(level, inner_carry):
            crossed = [[None, None], [None, None]]
            for t in range(2):
                for comp in range(2):
                    value = cur[slot, t, comp, level + 1]
                    slope = pltpu.roll(value, wide - 1, 0) - pltpu.roll(value, 1, 0)
                    crossed[comp][t] = (slope + slope)[kept]
            for comp in range(2):
                centre, ups, downs = [], [], []
                for t in range(2):
                    below = cur[slot, t, comp, level]
                    value = cur[slot, t, comp, level + 1]
                    above = cur[slot, t, comp, level + 2]
                    plain = smooth_rows(below + 2.0 * value + above)[kept]
                    scaled = smooth_rows(
                        eta[t, level] * below
                        + 2.0 * (eta[t, level + 1] * value)
                        + eta[t, level + 2] * above
                    )[kept]
                    cross = crossed[1 - comp][t]
                    centre.append(
                        (centre_coef[t, level, kept] - newton) * value[kept]
                        - (a_mid[t, level, kept] * plain + g_mid[t, level, kept] * scaled)
                    )
                    ups.append(a_up[t, level, kept] * (plain - cross) + g_up[t, level, kept] * scaled)
                    downs.append(a_down[t, level, kept] * (plain + cross) + g_down[t, level, kept] * scaled)
                after, before = from_next(*ups), from_last(*downs)
                for t in range(2):
                    result = centre[t] - (after[t] + before[t])
                    if not final:
                        cur[1 - slot, t, comp, level + 1] = result
                    if final and t == 0:
                        out_ref[power + 1, comp, level] = result
                    elif t == 0:
                        out_ref[power + 1, comp, level] = result[HALO : HALO + rows]
            return inner_carry

        return lax.fori_loop(0, levels, level_step, carry)

    lax.fori_loop(0, powers - 1, power_step, 0)
    power_step(powers - 1, 0, final=True)

    pairs = [(i, j) for i in range(count) for j in range(i + 1)]
    place = {pair: n for n, pair in enumerate(pairs)}
    tiles = (len(pairs) + 7) // 8
    lane_8 = lax.broadcasted_iota(jnp.int32, (8, lanes), 1)

    def add_products(sums, vectors):
        return tuple(total + vectors[i] * vectors[j] for total, (i, j) in zip(sums, pairs))

    zeros = tuple(jnp.zeros((8, lanes), jnp.float32) for _ in pairs)

    def exchange(phase, mine, slots, sends, recvs, me, peers, target):
        copies_out = []
        for step in range(1, peers):
            copy = pltpu.make_async_remote_copy(
                src_ref=mine.at[phase],
                dst_ref=slots.at[phase, me],
                send_sem=sends.at[phase, step],
                recv_sem=recvs.at[phase, step],
                device_id=target(step),
                device_id_type=MESH,
            )
            copy.start()
            copies_out.append(copy)
        slots[phase, me] = mine[phase]
        for copy in copies_out:
            copy.wait()
        total = slots[phase, 0]
        for peer in range(1, peers):
            total = total + slots[phase, peer]
        return total

    def gram_of(sums, phase):
        red[8 * tiles - 8 : 8 * tiles] = jnp.zeros((8, lanes), jnp.float32)
        for n, total in enumerate(sums):
            red[n : n + 1] = jnp.sum(total, axis=0, keepdims=True)
        summed = jnp.sum(red[...], axis=1, keepdims=True)
        tile = jnp.zeros((8, lanes), jnp.float32)
        for t in range(tiles):
            tile = jnp.where(lane_8 == t, summed[8 * t : 8 * t + 8], tile)
        mine_x[phase] = tile
        mine_y[phase] = exchange(
            phase, mine_x, slots_x, gx_send, gx_recv, me_x, gx_count, ring_x
        )
        whole = exchange(phase, mine_y, slots_y, gy_send, gy_recv, me_y, gy_count, ring_y)
        whole = whole / total_count
        for t in range(tiles):
            splat[8 * t : 8 * t + 8] = jnp.broadcast_to(whole[:, t : t + 1], (8, lanes))
        return {pair: splat[n : n + 1] for n, pair in enumerate(pairs)}

    def factorise(gram):
        left = dict(gram)
        low, inv = {}, {}
        for j in range(count):
            root = jnp.sqrt(left[j, j])
            scale = 1.0 / root
            low[j, j], inv[j, j] = root, scale
            for i in range(j + 1, count):
                low[i, j] = left[i, j] * scale
            for i in range(j + 1, count):
                for k in range(j + 1, i + 1):
                    left[i, k] = left[i, k] - low[i, j] * low[k, j]
        for i in range(count):
            for j in range(i):
                total = low[i, j] * inv[j, j]
                for k in range(j + 1, i):
                    total = total + low[i, k] * inv[k, j]
                inv[i, j] = -(total * inv[i, i])
        for pair, n in place.items():
            lower_inv[n : n + 1] = inv[pair]
        return low

    def combine(vectors):
        results = []
        for i in range(count):
            total = lower_inv[place[i, 0] : place[i, 0] + 1] * vectors[0]
            for j in range(1, i + 1):
                total = total + lower_inv[place[i, j] : place[i, j] + 1] * vectors[j]
            results.append(total)
        return results

    def basis_at(spot, half):
        comp, level = spot // levels, lax.rem(spot, levels)
        return [out_ref[n, comp, level, 8 * half : 8 * half + 8] for n in range(count)]

    def gram_step(spot, sums):
        for half in range(rows // 8):
            sums = add_products(sums, basis_at(spot, half))
        return sums

    low_one = factorise(gram_of(lax.fori_loop(0, 2 * levels, gram_step, zeros), 0))

    def ortho_step(spot, sums):
        comp, level = spot // levels, lax.rem(spot, levels)
        for half in range(rows // 8):
            vectors = combine(basis_at(spot, half))
            for n in range(count):
                out_ref[n, comp, level, 8 * half : 8 * half + 8] = vectors[n]
            sums = add_products(sums, vectors)
        return sums

    low_two = factorise(gram_of(lax.fori_loop(0, 2 * levels, ortho_step, zeros), 1))

    def last_step(spot, carry):
        comp, level = spot // levels, lax.rem(spot, levels)
        for half in range(rows // 8):
            vectors = combine(basis_at(spot, half))
            for n in range(count):
                out_ref[n, comp, level, 8 * half : 8 * half + 8] = vectors[n]
        return carry

    lax.fori_loop(0, 2 * levels, last_step, 0)

    fac_row = lax.broadcasted_iota(jnp.int32, (count, count), 0)
    fac_col = lax.broadcasted_iota(jnp.int32, (count, count), 1)
    factor = jnp.zeros((count, count), jnp.float32)
    for i in range(count):
        for j in range(i, count):
            total = low_two[i, i] * low_one[j, i]
            for k in range(i + 1, j + 1):
                total = total + low_two[k, i] * low_one[j, k]
            factor = jnp.where((fac_row == i) & (fac_col == j), total[:, :count], factor)
    factor_ref[...] = factor

    for index, (dx, dy) in enumerate(DIRECTIONS):

        @pl.when(exists(dx, dy))
        def _():
            for copy in copies(index):
                copy.wait_send()


def on_device(gx_count, gy_count, start_vector, viscosity, friction, shifts):
    levels, rows, lanes = viscosity.shape
    count = shifts.shape[0] + 1
    wide = rows + 2 * HALO
    tiles = (count * (count + 1) // 2 + 7) // 8
    f32 = jnp.float32
    coef = pltpu.VMEM((2, levels, wide, lanes), f32)
    dma = pltpu.SemaphoreType.DMA
    vmem = pl.BlockSpec(memory_space=pltpu.VMEM)
    return pl.pallas_call(
        functools.partial(kernel, gx_count, gy_count),
        out_shape=(
            jax.ShapeDtypeStruct((count,) + start_vector.shape, f32),
            jax.ShapeDtypeStruct((count, count), f32),
        ),
        in_specs=[vmem, vmem, vmem, pl.BlockSpec(memory_space=pltpu.SMEM)],
        out_specs=(vmem, vmem),
        scratch_shapes=[
            pltpu.VMEM((2, 2, 2, levels + 2, wide, lanes), f32),
            pltpu.VMEM((2, levels + 2, wide, lanes), f32),
            coef,
            coef,
            coef,
            coef,
            coef,
            coef,
            coef,
            coef,
            pltpu.VMEM((levels // 2, rows, lanes), f32),
            pltpu.VMEM((2, levels // 2, wide, lanes), f32),
            pltpu.VMEM((8 * tiles, lanes), f32),
            pltpu.VMEM((2, 8, lanes), f32),
            pltpu.VMEM((2, 8, lanes), f32),
            pltpu.VMEM((2, gx_count, 8, lanes), f32),
            pltpu.VMEM((2, gy_count, 8, lanes), f32),
            pltpu.VMEM((8 * tiles, lanes), f32),
            pltpu.VMEM((8 * tiles, lanes), f32),
            dma((2, 3)),
            dma((2, 3)),
            dma((6,)),
            dma((6,)),
            dma((2, gx_count)),
            dma((2, gx_count)),
            dma((2, gy_count)),
            dma((2, gy_count)),
        ],
        compiler_params=pltpu.CompilerParams(
            collective_id=0, has_side_effects=True, vmem_limit_bytes=40 * 2**20
        ),
    )(start_vector, viscosity, friction, shifts)


def solution(mesh):
    return jax.shard_map(
        functools.partial(on_device, mesh.shape["gx"], mesh.shape["gy"]),
        mesh=mesh,
        in_specs=(P(None, None, "gx", "gy"), P(None, "gx", "gy"), P(None, "gx", "gy"), P()),
        out_specs=(P(None, None, None, "gx", "gy"), P()),
        check_vma=False,
    )
```

```python
import functools

import jax
import jax.numpy as jnp
from jax import lax
from jax.experimental import pallas as pl
from jax.experimental.pallas import tpu as pltpu
from jax.sharding import PartitionSpec as P

MESH = pl.DeviceIdType.MESH
HALO = 8
GROUP = 2 * HALO
DIRECTIONS = ((1, 0), (-1, 0), (0, 1), (0, -1), (1, 1), (1, -1), (-1, 1), (-1, -1))


def both(lower_ok, upper_ok):
    if lower_ok is None:
        return upper_ok
    if upper_ok is None:
        return lower_ok
    return jnp.logical_and(lower_ok, upper_ok)


def kernel(
    gx_count,
    gy_count,
    start_ref,
    eta_in_ref,
    fric_in_ref,
    shift_ref,
    out_ref,
    factor_ref,
    lower_inv,
    cur,
    eta,
    fric,
    centre_coef,
    a_mid,
    g_mid,
    a_up,
    g_up,
    a_down,
    g_down,
    packed,
    edge,
    red,
    mine_x,
    mine_y,
    slots_x,
    slots_y,
    splat,
    row_send,
    row_recv,
    pack_send,
    pack_recv,
    gx_send,
    gx_recv,
    gy_send,
    gy_recv,
):
    powers = shift_ref.shape[0]
    count = powers + 1
    levels, rows, lanes = eta_in_ref.shape
    wide = rows + 2 * HALO
    me_x, me_y = lax.axis_index("gx"), lax.axis_index("gy")
    total_count = 2.0 * levels * rows * lanes * gx_count * gy_count

    def exists(dx, dy):
        x_ok = {1: me_x < gx_count - 1, -1: me_x > 0, 0: None}[dx]
        y_ok = {1: me_y < gy_count - 1, -1: me_y > 0, 0: None}[dy]
        return both(x_ok, y_ok)

    def device(dx, dy):
        return (jnp.clip(me_x + dx, 0, gx_count - 1), jnp.clip(me_y + dy, 0, gy_count - 1))

    def ring_x(step):
        return (lax.rem(me_x + step, gx_count), me_y)

    def ring_y(step):
        return (me_x, lax.rem(me_y + step, gy_count))

    barrier = pltpu.get_barrier_semaphore()
    for step in range(1, gx_count):
        pl.semaphore_signal(barrier, inc=1, device_id=ring_x(step), device_id_type=MESH)
    for step in range(1, gy_count):
        pl.semaphore_signal(barrier, inc=1, device_id=ring_y(step), device_id_type=MESH)
    for dx, dy in DIRECTIONS[4:]:

        @pl.when(exists(dx, dy))
        def _():
            pl.semaphore_signal(barrier, inc=1, device_id=device(dx, dy), device_id_type=MESH)

    lane = lax.broadcasted_iota(jnp.int32, (wide, lanes), 1)
    row = lax.broadcasted_iota(jnp.int32, (wide, lanes), 0)
    lane_in = lane[:rows]

    def source(field, level):
        if field < 2:
            return start_ref[field, level]
        return (eta_in_ref, fric_in_ref)[field - 2][level]

    for field in range(4):
        for group in range(levels // 8):
            tile = jnp.zeros((rows, lanes), jnp.float32)
            for inner in range(8):
                turned = pltpu.roll(
                    source(field, group * 8 + inner), (GROUP * inner + HALO) % lanes, 1
                )
                tile = jnp.where(lane_in // GROUP == inner, turned, tile)
            packed[field * (levels // 8) + group] = tile

    barrier_x = jnp.where(me_x > 0, 1, 0) + jnp.where(me_x < gx_count - 1, 1, 0)
    barrier_y = jnp.where(me_y > 0, 1, 0) + jnp.where(me_y < gy_count - 1, 1, 0)
    pl.semaphore_wait(barrier, gx_count + gy_count - 2 + barrier_x * barrier_y)

    def row_copies(index):
        dx, dy = DIRECTIONS[index]
        src = pl.ds(rows - HALO, HALO) if dx > 0 else pl.ds(0, HALO)
        dst = pl.ds(0, HALO) if dx > 0 else pl.ds(rows + HALO, HALO)
        inner = pl.ds(1, levels)
        pairs = (
            (start_ref.at[:, :, src], cur.at[0, 0, :, inner, dst]),
            (eta_in_ref.at[:, src], eta.at[0, inner, dst]),
            (fric_in_ref.at[:, src], fric.at[0, :, dst]),
        )
        return [
            pltpu.make_async_remote_copy(
                src_ref=a,
                dst_ref=b,
                send_sem=row_send.at[index, n],
                recv_sem=row_recv.at[index, n],
                device_id=device(dx, dy),
                device_id_type=MESH,
            )
            for n, (a, b) in enumerate(pairs)
        ]

    def pack_copies(index):
        dx, dy = DIRECTIONS[index]
        side = 0 if dy > 0 else 1
        if dx == 0:
            src, dst = pl.ds(0, rows), pl.ds(HALO, rows)
        elif dx > 0:
            src, dst = pl.ds(rows - HALO, HALO), pl.ds(0, HALO)
        else:
            src, dst = pl.ds(0, HALO), pl.ds(rows + HALO, HALO)
        return [
            pltpu.make_async_remote_copy(
                src_ref=packed.at[:, src],
                dst_ref=edge.at[side, :, dst],
                send_sem=pack_send.at[index - 2],
                recv_sem=pack_recv.at[index - 2],
                device_id=device(dx, dy),
                device_id_type=MESH,
            )
        ]

    def copies(index):
        return row_copies(index) if index < 2 else pack_copies(index)

    for index, (dx, dy) in enumerate(DIRECTIONS):

        @pl.when(exists(dx, dy))
        def _():
            for copy in copies(index):
                copy.start()

    zero_tile = jnp.zeros((wide, lanes), jnp.float32)
    for comp in range(2):
        for tile in range(2):
            for slot in range(2):
                cur[slot, tile, comp, 0] = zero_tile
                cur[slot, tile, comp, levels + 1] = zero_tile
        cur[0, 0, comp, 1 : levels + 1, HALO : HALO + rows] = start_ref[comp]
        out_ref[0, comp] = start_ref[comp]
    for tile in range(2):
        eta[tile, 0] = zero_tile
        eta[tile, levels + 1] = zero_tile
    eta[0, 1 : levels + 1, HALO : HALO + rows] = eta_in_ref[...]
    fric[0, :, HALO : HALO + rows] = fric_in_ref[...]
    for index, (dx, dy) in enumerate(DIRECTIONS):
        here = exists(-dx, -dy)

        @pl.when(jnp.logical_not(here))
        def _():
            start = 0 if dx > 0 else (HALO if dx == 0 else rows + HALO)
            size = rows if dx == 0 else HALO
            if dy == 0:
                blank = jnp.zeros((levels, HALO, lanes), jnp.float32)
                for comp in range(2):
                    cur[0, 0, comp, 1 : levels + 1, start : start + size] = blank
                eta[0, 1 : levels + 1, start : start + size] = blank
                fric[0, :, start : start + size] = blank
            else:
                side = 0 if dy > 0 else 1
                edge[side, :, start : start + size] = jnp.zeros(
                    (edge.shape[1], size, lanes), jnp.float32
                )

        @pl.when(here)
        def _():
            for copy in copies(index):
                copy.wait_recv()

    is_edge = (lane < HALO) | (lane >= lanes - HALO)
    for field in range(4):
        for group in range(levels // 8):
            spot = field * (levels // 8) + group
            merged = jnp.where(lane % GROUP >= HALO, edge[1, spot], edge[0, spot])
            for inner in range(8):
                level = group * 8 + inner
                turned = pltpu.roll(merged, (2 * lanes - GROUP * inner - HALO) % lanes, 1)
                turned = jnp.where(is_edge, turned, 0.0)
                if field < 2:
                    cur[0, 1, field, level + 1] = turned
                elif field == 2:
                    eta[1, level + 1] = turned
                else:
                    fric[1, level] = turned

    def from_next(first, second):
        a, b = pltpu.roll(first, lanes - 1, 1), pltpu.roll(second, lanes - 1, 1)
        at_end = lane[: first.shape[0]] == lanes - 1
        return jnp.where(at_end, b, a), jnp.where(at_end, a, b)

    def from_last(first, second):
        a, b = pltpu.roll(first, 1, 1), pltpu.roll(second, 1, 1)
        at_start = lane[: first.shape[0]] == 0
        return jnp.where(at_start, b, a), jnp.where(at_start, a, b)

    def smooth_rows(value):
        pair = value + pltpu.roll(value, wide - 1, 0)
        return pair + pltpu.roll(pair, 1, 0)

    row_ok = ((row >= HALO) | (me_x > 0)) & ((row < HALO + rows) | (me_x < gx_count - 1))
    side_ok = ((lane < HALO) & (me_y < gy_count - 1)) | ((lane >= lanes - HALO) & (me_y > 0))
    inside = (row_ok, row_ok & side_ok)

    def coefficients(level, carry):
        sums = [
            smooth_rows(eta[t, level] + 2.0 * eta[t, level + 1] + eta[t, level + 2])
            for t in range(2)
        ]
        after, before = from_next(*sums), from_last(*sums)
        a_pair, g_pair = [], []
        for t in range(2):
            here = eta[t, level + 1]
            diagonal = (
                fric[t, level] + 6.0 * here + 0.125 * (2.0 * sums[t] + after[t] + before[t])
            )
            inverse = jnp.where(inside[t], 0.125 / jnp.where(inside[t], diagonal, 1.0), 0.0)
            a_pair.append(here * inverse)
            g_pair.append(inverse)
            centre_coef[t, level] = 1.0 + 16.0 * a_pair[t]
            a_mid[t, level] = 2.0 * a_pair[t]
            g_mid[t, level] = 2.0 * g_pair[t]
        for values, up, down in ((a_pair, a_up, a_down), (g_pair, g_up, g_down)):
            ahead, behind = from_last(*values), from_next(*values)
            for t in range(2):
                up[t, level] = ahead[t]
                down[t, level] = behind[t]
        return carry

    lax.fori_loop(0, levels, coefficients, 0)

    def power_step(power, carry, final=False):
        kept = slice(HALO, HALO + rows) if final else slice(0, wide)

        slot = power % 2
        newton = shift_ref[power]

        def level_step(level, inner_carry):
            crossed = [[None, None], [None, None]]
            for t in range(2):
                for comp in range(2):
                    value = cur[slot, t, comp, level + 1]
                    slope = pltpu.roll(value, wide - 1, 0) - pltpu.roll(value, 1, 0)
                    crossed[comp][t] = (slope + slope)[kept]
            for comp in range(2):
                centre, ups, downs = [], [], []
                for t in range(2):
                    below = cur[slot, t, comp, level]
                    value = cur[slot, t, comp, level + 1]
                    above = cur[slot, t, comp, level + 2]
                    plain = smooth_rows(below + 2.0 * value + above)[kept]
                    scaled = smooth_rows(
                        eta[t, level] * below
                        + 2.0 * (eta[t, level + 1] * value)
                        + eta[t, level + 2] * above
                    )[kept]
                    cross = crossed[1 - comp][t]
                    centre.append(
                        (centre_coef[t, level, kept] - newton) * value[kept]
                        - (a_mid[t, level, kept] * plain + g_mid[t, level, kept] * scaled)
                    )
                    ups.append(a_up[t, level, kept] * (plain - cross) + g_up[t, level, kept] * scaled)
                    downs.append(a_down[t, level, kept] * (plain + cross) + g_down[t, level, kept] * scaled)
                after, before = from_next(*ups), from_last(*downs)
                for t in range(2):
                    result = centre[t] - (after[t] + before[t])
                    if not final:
                        cur[1 - slot, t, comp, level + 1] = result
                    if final and t == 0:
                        out_ref[power + 1, comp, level] = result
                    elif t == 0:
                        out_ref[power + 1, comp, level] = result[HALO : HALO + rows]
            return inner_carry

        return lax.fori_loop(0, levels, level_step, carry)

    lax.fori_loop(0, powers - 1, power_step, 0)
    power_step(powers - 1, 0, final=True)

    pairs = [(i, j) for i in range(count) for j in range(i + 1)]
    place = {pair: n for n, pair in enumerate(pairs)}
    tiles = (len(pairs) + 7) // 8
    lane_8 = lax.broadcasted_iota(jnp.int32, (8, lanes), 1)

    def add_products(sums, vectors):
        return tuple(total + vectors[i] * vectors[j] for total, (i, j) in zip(sums, pairs))

    zeros = tuple(jnp.zeros((8, lanes), jnp.float32) for _ in pairs)

    def exchange(phase, mine, slots, sends, recvs, me, peers, target):
        copies_out = []
        for step in range(1, peers):
            copy = pltpu.make_async_remote_copy(
                src_ref=mine.at[phase],
                dst_ref=slots.at[phase, me],
                send_sem=sends.at[phase, step],
                recv_sem=recvs.at[phase, step],
                device_id=target(step),
                device_id_type=MESH,
            )
            copy.start()
            copies_out.append(copy)
        slots[phase, me] = mine[phase]
        for copy in copies_out:
            copy.wait()
        total = slots[phase, 0]
        for peer in range(1, peers):
            total = total + slots[phase, peer]
        return total

    def gram_of(sums, phase):
        red[8 * tiles - 8 : 8 * tiles] = jnp.zeros((8, lanes), jnp.float32)
        for n, total in enumerate(sums):
            red[n : n + 1] = jnp.sum(total, axis=0, keepdims=True)
        summed = jnp.sum(red[...], axis=1, keepdims=True)
        tile = jnp.zeros((8, lanes), jnp.float32)
        for t in range(tiles):
            tile = jnp.where(lane_8 == t, summed[8 * t : 8 * t + 8], tile)
        mine_x[phase] = tile
        mine_y[phase] = exchange(
            phase, mine_x, slots_x, gx_send, gx_recv, me_x, gx_count, ring_x
        )
        whole = exchange(phase, mine_y, slots_y, gy_send, gy_recv, me_y, gy_count, ring_y)
        whole = whole / total_count
        for t in range(tiles):
            splat[8 * t : 8 * t + 8] = jnp.broadcast_to(whole[:, t : t + 1], (8, lanes))
        return {pair: splat[n : n + 1] for n, pair in enumerate(pairs)}

    def factorise(gram):
        left = dict(gram)
        low, inv = {}, {}
        for j in range(count):
            root = jnp.sqrt(left[j, j])
            scale = 1.0 / root
            low[j, j], inv[j, j] = root, scale
            for i in range(j + 1, count):
                low[i, j] = left[i, j] * scale
            for i in range(j + 1, count):
                for k in range(j + 1, i + 1):
                    left[i, k] = left[i, k] - low[i, j] * low[k, j]
        for i in range(count):
            for j in range(i):
                total = low[i, j] * inv[j, j]
                for k in range(j + 1, i):
                    total = total + low[i, k] * inv[k, j]
                inv[i, j] = -(total * inv[i, i])
        for pair, n in place.items():
            lower_inv[n : n + 1] = inv[pair]
        return low

    def combine(vectors):
        results = []
        for i in range(count):
            total = lower_inv[place[i, 0] : place[i, 0] + 1] * vectors[0]
            for j in range(1, i + 1):
                total = total + lower_inv[place[i, j] : place[i, j] + 1] * vectors[j]
            results.append(total)
        return results

    def basis_at(spot, half):
        comp, level = spot // levels, lax.rem(spot, levels)
        return [out_ref[n, comp, level, 8 * half : 8 * half + 8] for n in range(count)]

    def gram_step(spot, sums):
        for half in range(rows // 8):
            sums = add_products(sums, basis_at(spot, half))
        return sums

    low_one = factorise(gram_of(lax.fori_loop(0, 2 * levels, gram_step, zeros), 0))

    def ortho_step(spot, sums):
        comp, level = spot // levels, lax.rem(spot, levels)
        for half in range(rows // 8):
            vectors = combine(basis_at(spot, half))
            for n in range(count):
                out_ref[n, comp, level, 8 * half : 8 * half + 8] = vectors[n]
            sums = add_products(sums, vectors)
        return sums

    low_two = factorise(gram_of(lax.fori_loop(0, 2 * levels, ortho_step, zeros), 1))

    fac_row = lax.broadcasted_iota(jnp.int32, (count, count), 0)
    fac_col = lax.broadcasted_iota(jnp.int32, (count, count), 1)
    factor = jnp.zeros((count, count), jnp.float32)
    for i in range(count):
        for j in range(i, count):
            total = low_two[i, i] * low_one[j, i]
            for k in range(i + 1, j + 1):
                total = total + low_two[k, i] * low_one[j, k]
            factor = jnp.where((fac_row == i) & (fac_col == j), total[:, :count], factor)
    factor_ref[...] = factor

    for index, (dx, dy) in enumerate(DIRECTIONS):

        @pl.when(exists(dx, dy))
        def _():
            for copy in copies(index):
                copy.wait_send()


def finish(inverse_ref, basis_ref, out_ref):
    count, _, depth, rows, _ = out_ref.shape
    comp, first = pl.program_id(0), pl.program_id(1) * depth

    def one_level(level, carry):
        for half in range(rows // 8):
            part = slice(8 * half, 8 * half + 8)
            vectors = [basis_ref[n, comp, first + level, part] for n in range(count)]
            spot = 0
            for i in range(count):
                total = inverse_ref[spot : spot + 1] * vectors[0]
                for j in range(1, i + 1):
                    total = total + inverse_ref[spot + j : spot + j + 1] * vectors[j]
                out_ref[i, 0, level, part] = total
                spot += i + 1
        return carry

    lax.fori_loop(0, depth, one_level, 0)


def on_device(gx_count, gy_count, start_vector, viscosity, friction, shifts):
    levels, rows, lanes = viscosity.shape
    count = shifts.shape[0] + 1
    wide = rows + 2 * HALO
    tiles = (count * (count + 1) // 2 + 7) // 8
    f32 = jnp.float32
    coef = pltpu.VMEM((2, levels, wide, lanes), f32)
    dma = pltpu.SemaphoreType.DMA
    vmem = pl.BlockSpec(memory_space=pltpu.VMEM)
    ortho_one, factor, inverse = pl.pallas_call(
        functools.partial(kernel, gx_count, gy_count),
        out_shape=(
            jax.ShapeDtypeStruct((count,) + start_vector.shape, f32),
            jax.ShapeDtypeStruct((count, count), f32),
            jax.ShapeDtypeStruct((8 * tiles, lanes), f32),
        ),
        in_specs=[vmem, vmem, vmem, pl.BlockSpec(memory_space=pltpu.SMEM)],
        out_specs=(vmem, vmem, vmem),
        scratch_shapes=[
            pltpu.VMEM((2, 2, 2, levels + 2, wide, lanes), f32),
            pltpu.VMEM((2, levels + 2, wide, lanes), f32),
            coef,
            coef,
            coef,
            coef,
            coef,
            coef,
            coef,
            coef,
            pltpu.VMEM((levels // 2, rows, lanes), f32),
            pltpu.VMEM((2, levels // 2, wide, lanes), f32),
            pltpu.VMEM((8 * tiles, lanes), f32),
            pltpu.VMEM((2, 8, lanes), f32),
            pltpu.VMEM((2, 8, lanes), f32),
            pltpu.VMEM((2, gx_count, 8, lanes), f32),
            pltpu.VMEM((2, gy_count, 8, lanes), f32),
            pltpu.VMEM((8 * tiles, lanes), f32),
            dma((2, 3)),
            dma((2, 3)),
            dma((6,)),
            dma((6,)),
            dma((2, gx_count)),
            dma((2, gx_count)),
            dma((2, gy_count)),
            dma((2, gy_count)),
        ],
        compiler_params=pltpu.CompilerParams(
            collective_id=0, has_side_effects=True, vmem_limit_bytes=40 * 2**20
        ),
    )(start_vector, viscosity, friction, shifts)
    depth = 8 if levels % 8 == 0 else 1
    block = pl.BlockSpec((count, 1, depth, rows, lanes), lambda c, z: (0, c, z, 0, 0))
    orthonormal = pl.pallas_call(
        finish,
        grid=(2, levels // depth),
        out_shape=jax.ShapeDtypeStruct(ortho_one.shape, f32),
        in_specs=[vmem, vmem],
        compiler_params=pltpu.CompilerParams(vmem_limit_bytes=12 * 2**20),
        out_specs=block,
    )(inverse, ortho_one)
    return orthonormal, factor


def solution(mesh):
    return jax.shard_map(
        functools.partial(on_device, mesh.shape["gx"], mesh.shape["gy"]),
        mesh=mesh,
        in_specs=(P(None, None, "gx", "gy"), P(None, "gx", "gy"), P(None, "gx", "gy"), P()),
        out_specs=(P(None, None, None, "gx", "gy"), P()),
        check_vma=False,
    )
```
